1024 devices in a mesh: dp: 32 (over z_lo, y), seq: 32 (over x, z_hi, core).
Axes of the slice: x: 4, y: 4, z: 32 (z_hi: 4, z_lo: 8; z = z_hi * 8 + z_lo), core: 2. Of those that a mesh axis runs over, the one named last changes fastest.
Arguments:
- attention_out: bfloat16 [131072, 1152], P(('dp', 'seq')), may hold values from -24 to 24
- upstream: bfloat16 [131072, 1152], P(('dp', 'seq')), may hold values from -6 to 6
- tap_slots: bfloat16 [3, 65536, 4608], P(None, ('dp', 'seq')), may hold values from -6 to 6
- owner_map: int32 [32768, 1], P(('dp', 'seq')), may hold values from 0 to 31; in each aligned block of 32 rows (0 to 31, 32 to 63, ...) at most 2 rows name the same one
- out_proj: bfloat16 [1152, 1152], replicated, may hold values from -0.1875 to 0.1875
Outputs:
- stream_grad: bfloat16 [131072, 1152], P(('dp', 'seq'))
- attention_grad: bfloat16 [131072, 1152], P(('dp', 'seq'))
- shallow_grads: bfloat16 [2, 131072, 1152], P(None, ('dp', 'seq'))
- proj_grad: float32 [1152, 1152], P('dp', 'seq')
The draws below stay inside these ranges and needn't reach their ends.
Inputs may be any that keep to these rules, and one draw needn't show every extreme that they name: `owner_map`: within the 32 merged tokens of one device no owner is named more than 2 times, a bound that some block reaches.
All inputs are finite; a program needn't handle non-finite values.
Results may differ from the reference program's by a relative error of at most 0.0051.
Values may be sent and summed in bfloat16 or wider, within the bound.
No kernel may reach another device: no remote copies, remote signals or barrier semaphores. Data moves between devices by JAX's collectives and lax.ppermute only.
A program may use at most 64 MiB of HBM per device.

```python
import math
import jax
import jax.numpy as jnp
import numpy as np
from jax import lax

D = 1152
MERGE = 4
LEVELS = 3
M_DEV = 32
CAP = 2
TOKENS = 131072
N_DP = 32
N_SEQ = 32


def spiked(entries, rng, source, target, shards_of, factor):
    def block_of(position):
        return (jnp.arange(entries.shape[position]) // (entries.shape[position] // shards_of)).reshape((-1,) + (1,) * (entries.ndim - 1 - position))

    first = jax.random.permutation(rng, shards_of)[block_of(target)]
    second = (block_of(target) + shards_of // 2) % shards_of
    return jnp.where((block_of(source) == first) | (block_of(source) == second), factor * entries, entries)


def level_of(key, shape, shards, low, high):
    loudness, own = 1.0, jax.random.fold_in(key, 6)
    for position, blocks in shards:
        draws = jnp.exp(jax.random.uniform(jax.random.fold_in(own, position), (blocks,), jnp.float32, low / len(shards), high / len(shards)))
        loudness = loudness * jnp.repeat(draws, shape[position] // blocks).reshape([-1 if axis == position else 1 for axis in range(len(shape))])
    return loudness


def shared_out(rng, own, number, rows, amount, top, bound, skew):
    sequence = jax.random.permutation(rng, amount)
    heavy_load, usual = shares(amount, rows * top, bound, skew, True), shares(amount, rows * top, bound, skew, False)
    places = jnp.arange(amount)

    def named(tallies, turn):
        used = int((tallies > 0).sum())
        fixed = max(1, used // 4)
        passed = fixed + (places - fixed + turn * (used - fixed)) % max(1, amount - fixed)
        return jnp.zeros((amount,), jnp.int32).at[sequence[jnp.where(places < fixed, places, passed)]].set(jnp.asarray(tallies, jnp.int32))

    tallies = jnp.where(number % 4 == 0, named(heavy_load, number // 4), named(usual, number - number // 4 - 1))
    mixed = jax.random.permutation(jax.random.fold_in(own, 3), amount)
    source_of, sink = mixed[0:amount // 2 * 2:2], mixed[1:amount // 2 * 2:2]
    room = jnp.minimum(tallies[source_of] - 1, bound - tallies[sink]) // 2
    room = jnp.where((source_of == sequence[0]) | (sink == sequence[0]) | (tallies[sink] == 0), 0, jnp.maximum(room, 0))
    passed = jax.random.randint(jax.random.fold_in(own, 4), (amount // 2,), 0, 1 << 20) % (room + 1)
    tallies = tallies.at[source_of].add(-passed).at[sink].add(passed)
    items = jnp.searchsorted(jnp.cumsum(tallies), jnp.arange(rows * top), side="right").astype(jnp.int32)
    grid = items.reshape(top, rows).T
    grid = grid[jax.random.permutation(jax.random.fold_in(own, 1), rows)]
    turn = jax.random.randint(jax.random.fold_in(own, 2), (rows, 1), 0, top)
    return jnp.take_along_axis(grid, (jnp.arange(top)[None, :] + turn) % top, axis=1)


def shares(number_of, total, most, lean, full):
    loads = [(1 << 20) // math.isqrt(grade ** lean) + 1 for grade in range(1, number_of + 1)]
    largest = most if full else min(most, max(-(-total // number_of), total * loads[0] // sum(loads)))
    least = 1 if total - largest >= number_of - 1 else 0
    given, spare = [largest] + [least] * (number_of - 1), total - largest - least * (number_of - 1)
    while spare > 0:
        free = [i for i in range(1, number_of) if given[i] < largest] or [i for i in range(1, number_of) if given[i] < most]
        mass, remaining = sum([loads[i] for i in free]), spare
        for i in free:
            more = min(most - given[i], max(1, remaining * loads[i] // mass), spare)
            given[i] = given[i] + more
            spare = spare - more
    return np.array(given)


def normal_values(own_key, dims, spread, reach, cuts=(), kind=jnp.bfloat16):
    level = level_of(own_key, dims, cuts, -0.22, 0.18) if cuts else 1.0
    entries = jax.random.normal(own_key, dims, jnp.float32) * spread * level
    return jnp.minimum(jnp.maximum(entries, -reach), reach).astype(kind)


def heavy_noise(stream_key, extent, width, most, shards, heavy, kind=jnp.bfloat16):
    values = width * jax.random.normal(stream_key, extent, jnp.float32)
    if shards:
        values = values * level_of(stream_key, extent, shards, -0.22, 0.18)
    return jnp.clip(spiked(values, jax.random.fold_in(stream_key, 3), *heavy), -most, most).astype(kind)


def setup_inputs(seed: int = 0) -> dict:
    arg_keys = jax.random.split(jax.random.key(seed), 6)
    attention_out = heavy_noise(arg_keys[0], (TOKENS, D), 1.0, 24.0, ((0, 1024),), (0, 1, 128, 5.5))
    upstream = normal_values(arg_keys[1], (TOKENS, D), 1.0, 6.0, ((0, 1024),))
    tap_slots = normal_values(arg_keys[2], (LEVELS, N_DP * N_SEQ * N_SEQ * CAP, MERGE * D), 1.0, 6.0, ((1, 1024),))
    owner_map_keys = jax.random.split(jax.random.fold_in(arg_keys[3], 1), (N_DP * N_SEQ * M_DEV) // M_DEV)
    owner_map_turns = jax.random.permutation(jax.random.fold_in(arg_keys[3], 3), (N_DP * N_SEQ * M_DEV) // M_DEV)
    owner_map = jax.vmap(lambda own, number: shared_out(jax.random.fold_in(arg_keys[3], 2), own, number, M_DEV, N_SEQ, 1, CAP, 2))(owner_map_keys, owner_map_turns).reshape((N_DP * N_SEQ * M_DEV, 1))
    out_proj = normal_values(arg_keys[4], (D, D), D ** -0.5, 0.1875)
    return dict(attention_out=attention_out, upstream=upstream, tap_slots=tap_slots, owner_map=owner_map, out_proj=out_proj)


def reference(attention_out, upstream, tap_slots, owner_map, out_proj):
    owners = owner_map[:, 0].reshape(N_DP * N_SEQ, M_DEV).astype(jnp.int32)
    onehot = (owners[:, :, None] == jnp.arange(N_SEQ, dtype=jnp.int32)[None, None, :]).astype(jnp.int32)
    before = (jnp.cumsum(onehot, axis=1) - onehot).astype(jnp.int32)
    rank = lax.optimization_barrier(jnp.sum(before * onehot, axis=2)).astype(jnp.int32)
    device = jnp.arange(N_DP * N_SEQ, dtype=jnp.int32)
    dp_index = device // N_SEQ
    seq_index = device % N_SEQ
    slot_row = ((dp_index[:, None] * N_SEQ + owners) * N_SEQ + seq_index[:, None]) * CAP + rank
    picked = jnp.take(tap_slots, slot_row.reshape(-1).astype(jnp.int32), axis=1)
    taps = picked.reshape(LEVELS, TOKENS, D)
    stream = (upstream.astype(jnp.float32) + taps[LEVELS - 1].astype(jnp.float32)).astype(jnp.bfloat16)
    attention_grad = lax.dot_general(stream, out_proj, (((1,), (1,)), ((), ())), preferred_element_type=jnp.float32).astype(jnp.bfloat16)
    proj_grad = lax.dot_general(attention_out, stream, (((0,), (0,)), ((), ())), preferred_element_type=jnp.float32)
    proj_grad = proj_grad * jnp.float32(1.0 / math.sqrt(TOKENS))
    return (stream, attention_grad, taps[0:LEVELS - 1], proj_grad)
```

```python
import functools
import math

import jax
import jax.numpy as jnp
import numpy as np
from jax import lax
from jax.experimental import pallas as pl
from jax.experimental.pallas import tpu as pltpu
from jax.sharding import Mesh
from jax.sharding import PartitionSpec as P

ZL, Y, X, ZH, C = 8, 4, 4, 4, 2
AXES = ("zl", "y", "x", "zh", "c")
MERGE = 4
M = 32
PATCHES = M * MERGE
SOURCES = X * C
SLOTS = 2 * SOURCES
BASE = 10
REST = SLOTS - BASE
KB = MERGE * BASE
KR = MERGE * REST
HELD = MERGE * ZH * 2
ROWS = SOURCES * HELD
FULL = SOURCES * MERGE * 2
TAIL = 16
GROUPS, UNIT, UPAD = 3, 12, 16
BF = jnp.bfloat16
F32 = jnp.float32


def vmem():
    return pl.BlockSpec(memory_space=pltpu.VMEM)


def smem():
    return pl.BlockSpec(memory_space=pltpu.SMEM)


def nt(a, b):
    return lax.dot_general(a, b, (((1,), (1,)), ((), ())), preferred_element_type=F32)


def nn(a, b):
    return lax.dot_general(a, b, (((1,), (0,)), ((), ())), preferred_element_type=F32)


def iota(shape, dim):
    return lax.broadcasted_iota(jnp.int32, shape, dim)


def ones_where(mask):
    return jnp.where(mask, 1.0, 0.0).astype(BF)


def like(*shape, dtype=BF):
    return jax.ShapeDtypeStruct(shape, dtype)


def call(kernel, out, *args, scratch=()):
    several = isinstance(out, list)
    return pl.pallas_call(
        kernel,
        in_specs=[smem() if a.ndim == 1 else vmem() for a in args],
        out_specs=[vmem()] * len(out) if several else vmem(),
        out_shape=out,
        scratch_shapes=scratch,
        compiler_params=pltpu.CompilerParams(vmem_limit_bytes=32 << 20),
    )(*args)


def plane(o):
    return (o >> 1) & 3


def within(o):
    return ((o >> 3) << 1) + (o & 1)


def regroup_kernel(at, in_ref, *outs):
    width = outs[0].shape[-1]
    q, s = iota((ROWS, 64), 0), iota((ROWS, 64), 1)
    x, c = ((q >> 6) + at[0]) & 3, ((q >> 5) & 1) ^ at[1]
    source = (x << 4) + (((q >> 1) & 3) << 2) + (c << 1) + (q & 1)
    total = jnp.zeros((ROWS, width), F32)
    for k in range(MERGE):
        pick = ones_where((source == s) & (((q >> 3) & 3) == k))
        total += nn(pick, in_ref[0, :, k * width : (k + 1) * width])
    total = total.astype(BF)
    if len(outs) == 1:
        outs[0][...] = total.reshape(outs[0].shape)
    else:
        for i, out in enumerate(outs):
            out[...] = total[i * HELD : (i + 1) * HELD].reshape(out.shape)


def regroup(at, tap_slots, first, levels, width, apart):
    if apart:
        out = [like(levels, HELD, width)] * SOURCES
        specs = [pl.BlockSpec((1, HELD, width), lambda i: (i, 0, 0))] * SOURCES
    else:
        out = like(SOURCES, levels, HELD, width)
        specs = pl.BlockSpec((SOURCES, 1, HELD, width), lambda i: (0, i, 0, 0))
    return pl.pallas_call(
        regroup_kernel,
        grid=(levels,),
        in_specs=[smem(), pl.BlockSpec((1, 64, MERGE * width), lambda i: (first + i, 0, 0))],
        out_specs=specs,
        out_shape=out,
    )(at, tap_slots)


def deep_kernel(held, owners, out_ref):
    q, s = iota((ROWS, ROWS), 0), iota((ROWS, ROWS), 1)
    order = (((q >> 3) & 7) << 5) + (((q >> 1) & 3) << 3) + ((q >> 6) << 1) + (q & 1)
    rows = nn(ones_where(order == s), held[...].reshape(ROWS, held.shape[-1])).astype(BF)
    for zh in range(ZH):
        for j in range(rows.shape[1] // 128):
            out_ref[zh, j * FULL : (j + 1) * FULL, :] = rows[zh * FULL : (zh + 1) * FULL, j * 128 : (j + 1) * 128]
        last = rows.shape[1] // 128 * FULL
        out_ref[zh, last : last + TAIL, :] = jnp.broadcast_to(owners[...], (TAIL, 128)).astype(BF)


def own_kernel(owners, out_ref):
    patch, token = iota((PATCHES, 128), 0), iota((PATCHES, 128), 1)
    row = jnp.broadcast_to(owners[...].astype(jnp.int32), (PATCHES, 128))
    mine = token == (patch >> 2)
    o = jnp.sum(jnp.where(mine, row, 0), axis=1, keepdims=True)
    rank = jnp.sum(jnp.where((token < (patch >> 2)) & (row == o), 1, 0), axis=1, keepdims=True)
    at = (within(o) << 3) + ((iota((PATCHES, FULL), 0) & 3) << 1) + rank
    for zh in range(ZH):
        out_ref[zh] = ones_where((plane(o) == zh) & (at == iota((PATCHES, FULL), 1)))


def stream_kernel(at, take, got, upstream, out_ref, *turned):
    tap = []
    for j in range(upstream.shape[1] // 128):
        total = nn(take[0], got[0, j * FULL : (j + 1) * FULL, :])
        for zh in range(1, ZH):
            total += nn(take[zh], got[zh, j * FULL : (j + 1) * FULL, :])
        tap.append(total)
    scratch = turned[-1]
    for j, total in enumerate(tap):
        part = (upstream[:, j * 128 : (j + 1) * 128].astype(F32) + total).astype(BF)
        out_ref[:, j * 128 : (j + 1) * 128] = part
        scratch[j * 128 : (j + 1) * 128, :] = part.astype(F32).T.astype(BF)
    rows = scratch.shape[0] // X
    for d, out in enumerate(turned[:-1]):
        first = pl.multiple_of(((at[0] + d) & 3) * rows, 32)
        out[...] = scratch[pl.ds(first, rows), :]


def list_tables():
    table = np.zeros((8, ZH * (KB + KR)), np.int32)
    for first, count, start in ((0, BASE, 0), (BASE, REST, ZH * KB)):
        q = np.arange(ZH * MERGE * count)
        at = slice(start, start + q.size)
        table[0, at] = q // (MERGE * count)
        table[1, at] = q // count % MERGE
        table[2, at] = first + q % count
    return table


def route_kernel(at, got, table_ref, column_ref, pack_base, pack_rest, take_base, take_rest, over_ref):
    tokens = ZH * M
    here = at[2]
    last = got.shape[1] - TAIL
    lane = iota((TAIL, tokens), 1) >> 5
    owners = jnp.zeros((TAIL, tokens), F32)
    for zh in range(ZH):
        owners = jnp.where(lane == zh, got[zh, last : last + TAIL, :].astype(F32), owners)
    owners = owners[0:1].astype(jnp.int32)
    t_row, t_col = iota((tokens, tokens), 1), iota((tokens, tokens), 0)
    o_row = jnp.broadcast_to(owners, (tokens, tokens))
    o_col_1 = jnp.sum(jnp.where(t_row == t_col, o_row, 0), axis=1, keepdims=True)
    o_col = jnp.broadcast_to(o_col_1, (tokens, tokens))
    mates = (t_row >> 5) == (t_col >> 5)
    listed = mates & (plane(o_row) == plane(o_col))
    s_row, s_col = within(o_row), within(o_col)
    col_before = listed & ((s_row < s_col) | ((s_row == s_col) & (t_row < t_col)))
    row_before = listed & ((s_col < s_row) | ((s_col == s_row) & (t_col < t_row)))
    place_col = jnp.sum(jnp.where(col_before, 1, 0), axis=1, keepdims=True)
    place_row = jnp.sum(jnp.where(row_before, 1, 0), axis=0, keepdims=True)
    rank_col = jnp.sum(jnp.where(mates & (o_row == o_col) & (t_row < t_col), 1, 0), axis=1, keepdims=True)
    over_ref[...] = jnp.broadcast_to(jnp.max(place_row, axis=1, keepdims=True), over_ref.shape)

    n, nb = ZH * (KB + KR), ZH * KB
    entry = ones_where(
        (column_ref[:, 0:1] == (iota((n, tokens), 1) >> 5)) & (column_ref[:, 2:3] == place_row) & (plane(owners) == here)
    )
    row = iota((tokens, HELD), 1)
    held = (((row >> 1) & 3) == (iota((tokens, HELD), 0) >> 5)) & ((row & 1) == rank_col)
    same_k = column_ref[:, 1:2] == (iota((n, HELD), 1) >> 3)
    for source in range(SOURCES):
        pick = nn(entry, ones_where(held & (within(o_col_1) == source)))
        pick = jnp.where(same_k, pick, 0.0).astype(BF)
        pack_base[source] = pick[:nb]
        pack_rest[source] = pick[nb:]
    mine = ones_where(iota((PATCHES, tokens), 1) == here * M + (iota((PATCHES, tokens), 0) >> 2))

    def take(zh, first, count):
        q = table_ref[:, first : first + count]
        taken = nn(mine, ones_where((plane(o_col_1) == zh) & (q[2:3, :] == place_col)))
        return jnp.where(q[1:2, :] == (iota((PATCHES, count), 0) & 3), taken, 0.0).astype(BF)

    for zh in range(ZH):
        take_base[zh] = take(zh, zh * KB, KB)
        take_rest[zh] = take(zh, nb + zh * KR, KR)


def route(at, got):
    table = list_tables()
    out = [
        like(SOURCES, ZH * KB, HELD),
        like(SOURCES, ZH * KR, HELD),
        like(ZH, PATCHES, KB),
        like(ZH, PATCHES, KR),
        like(8, 128, dtype=jnp.int32),
    ]
    return call(route_kernel, out, at, got, jnp.asarray(table), jnp.asarray(table.T))


def pack_kernel(level, at, picks, *refs):
    held, out = refs[:-1], refs[-1]
    total = None
    for i, ref in enumerate(held):
        source = (((at[0] - (i >> 1)) & 3) << 1) + ((i & 1) ^ at[1])
        part = nn(picks[source], ref[level])
        total = part if total is None else total + part
    rows = out.shape[1]
    for zh in range(ZH):
        out[zh] = total[zh * rows : (zh + 1) * rows].astype(BF)


def pack(at, picks, held, level):
    out = like(ZH, picks.shape[1] // ZH, held[0].shape[-1])
    return call(functools.partial(pack_kernel, level), out, at, picks, *held)


def shallow_kernel(take_base, take_rest, got0, got1, rest, out_ref):
    width = out_ref.shape[-1]
    for level, got in enumerate((got0, got1)):
        tap = jnp.zeros((PATCHES, width), F32)
        for zh in range(ZH):
            tap += nn(take_base[zh], got[zh, :, :width])
            tap += nn(take_rest[zh], rest[level, zh])
        out_ref[level] = tap.astype(BF)


def partial_kernel(at, a0, a1, a2, a3, s0, s1, s2, s3, place, mine, other, scratch):
    total = nt(a0[...], s0[...])
    for a, s in ((a1, s1), (a2, s2), (a3, s3)):
        total += nt(a[...], s[...])
    scratch[...] = total.astype(BF)
    rows = ZL * UPAD
    for d in range(Y):
        y = (at[3] + d) & 3
        block = None
        for g in range(GROUPS):
            first = pl.multiple_of((y * GROUPS + g) * rows, rows)
            part = nn(scratch[pl.ds(first, rows), :], place[g])
            block = part if block is None else block + part
        low, high = block[:, : ZH * 128], block[:, ZH * 128 :]
        first_core = at[1] == 0
        ours, theirs = jnp.where(first_core, low, high), jnp.where(first_core, high, low)
        for zh in range(ZH):
            mine[d, zh] = ours[:, zh * 128 : (zh + 1) * 128]
            other[d, zh] = theirs[:, zh * 128 : (zh + 1) * 128].astype(BF)


def sum_c_kernel(mine, got, own, *outs):
    own[...] = mine[0] + got[0].astype(F32)
    for d, out in enumerate(outs, 1):
        out[...] = (mine[d] + got[d].astype(F32)).astype(BF)


def sum_y_kernel(own, g1, g2, g3, out_ref):
    total = own[...] + g1[...].astype(F32) + g2[...].astype(F32) + g3[...].astype(F32)
    for zl in range(ZL):
        out_ref[zl] = total[:, zl * UPAD : (zl + 1) * UPAD, :].astype(BF)


def join_kernel(parts, rows, out_ref):
    width = rows.shape[-1]
    total = parts[0].astype(F32)
    for i in range(1, ZL):
        total += parts[i].astype(F32)
    out_ref[:, :, :width] = rows[...]
    out_ref[:, :UPAD, width:] = total.astype(BF)
    out_ref[:, UPAD:, width:] = jnp.zeros((ZH, rows.shape[1] - UPAD, 128), BF)


def final_kernel(factor, got, out_ref):
    width = got.shape[-1] - 128
    total = got[0, :UPAD, width:].astype(F32)
    for i in range(1, ZH):
        total += got[i, :UPAD, width:].astype(F32)
    total = total * factor
    for g in range(GROUPS):
        out_ref[g * UNIT : (g + 1) * UNIT, :] = total[:UNIT, g * 36 : (g + 1) * 36]


def after(x, *earlier):
    return lax.optimization_barrier((x, *earlier))[0]


def exchange(x, axes):
    return lax.all_to_all(x, axes, 0, 0, tiled=True)


def shift(x, axis, by):
    n = lax.axis_size(axis)
    return lax.ppermute(x, axis, [(i, (i + by) % n) for i in range(n)])


def shift_xc(x, i):
    dx, dc = i >> 1, i & 1
    return lax.ppermute(x, ("x", "c"), [(a * C + b, (a + dx) % X * C + (b ^ dc)) for a in range(X) for b in range(C)])


def on_device(attention_out, upstream, tap_slots, owner_map, out_proj):
    width = attention_out.shape[1]
    factor = 1.0 / math.sqrt(PATCHES * ZL * Y * X * ZH * C)
    at = jnp.stack([lax.axis_index(a) for a in ("x", "c", "zh", "y")]).astype(jnp.int32)
    owners = jnp.tile(owner_map.reshape(1, M), (1, ZH)).astype(F32)

    q = np.arange(Y * GROUPS * ZL * UPAD)
    u, zl, g, y = q % UPAD, q // UPAD % ZL, q // (UPAD * ZL) % GROUPS, q // (UPAD * ZL * GROUPS)
    r_of = np.where(u < UNIT, zl * 144 + y * 36 + g * UNIT + u, -1)
    select = (jnp.asarray(r_of, jnp.int32)[:, None] == jnp.arange(width, dtype=jnp.int32)[None, :]).astype(BF)
    a_t = nt(select, attention_out).astype(BF)
    i, n = np.arange(288)[:, None], np.arange(C * ZH * 128)[None, :]
    j = [n % 128 - 36 * g for g in range(GROUPS)]
    place = np.stack([(i == (n // 128 % ZH) * 72 + (n // 512) * 36 + e) & (e >= 0) & (e < 36) for e in j])
    place = jnp.asarray(place.astype(np.float32), BF)

    held2 = exchange(regroup(jnp.zeros((4,), jnp.int32), tap_slots, 2, 1, width, False), ("x", "c"))
    take2 = call(own_kernel, like(ZH, PATCHES, FULL), owners)
    got2 = exchange(call(deep_kernel, like(ZH, width // 128 * FULL + TAIL, 128), held2, owners), "zh")
    held01 = [after(part, held2) for part in regroup(at, tap_slots, 0, 2, width, True)]
    held01 = [held01[0]] + [shift_xc(part, i) for i, part in enumerate(held01) if i]
    a_t = after(a_t, held2)
    a_from = [a_t] + [shift(a_t, "x", d) for d in (1, 2, 3)]

    pack_base, pack_rest, take_base, take_rest, over = route(after(at, take2, *a_from), got2)
    overflow = over[0, 0] >= BASE
    got0 = exchange(pack(at, pack_base, held01, 0), "zh")
    packed1 = pack(at, pack_base, held01, 1)

    turned = [like(width // X, PATCHES)] * X
    stream, *turned = call(
        stream_kernel, [like(PATCHES, width), *turned], at, take2, got2, upstream, scratch=[pltpu.VMEM((width, PATCHES), BF)]
    )
    s_from = [turned[0]] + [shift(turned[d], "x", d) for d in (1, 2, 3)]
    attention_grad = nt(stream, out_proj).astype(BF)
    block = (Y, ZH, ZL * UPAD, 128)
    mine, other = call(
        partial_kernel,
        [like(*block, dtype=F32), like(*block)],
        at,
        *a_from,
        *s_from,
        place,
        scratch=[pltpu.VMEM((a_t.shape[0], width // X), BF)],
    )
    own, *parts = call(sum_c_kernel, [like(*block[1:], dtype=F32)] + [like(*block[1:])] * 3, mine, shift(other, "c", 1))
    parts = [shift(part, "y", d) for d, part in enumerate(parts, 1)]
    partial = call(sum_y_kernel, like(ZL, ZH, UPAD, 128), own, *parts)
    partial = exchange(after(partial, got0), "zl")
    got1 = exchange(call(join_kernel, like(ZH, KB, width + 128), partial, packed1), "zh")
    proj_grad = call(functools.partial(final_kernel, factor), like(36, 36, dtype=F32), got1)

    def second(picks, *held):
        return jnp.stack([exchange(pack(at, picks, held, level), "zh") for level in (0, 1)])

    rest = lax.cond(
        overflow, second, lambda picks, *held: jnp.zeros((2, ZH, KR, width), BF), after(pack_rest, got1), *held01
    )
    shallow = call(shallow_kernel, like(2, PATCHES, width), take_base, take_rest, got0, got1, rest)
    return (stream, attention_grad, shallow, proj_grad)


def solution(mesh):
    fine = Mesh(mesh.devices.reshape(ZL, Y, X, ZH, C), AXES)
    dp, seq = ("zl", "y"), ("x", "zh", "c")
    in_specs = (P(AXES, None), P(AXES, None), P(None, AXES, None), P(AXES, None), P())
    out_specs = (P(AXES, None), P(AXES, None), P(None, AXES, None), P(dp, seq))
    return jax.shard_map(on_device, mesh=fine, in_specs=in_specs, out_specs=out_specs, check_vma=False)
```

```python
import functools
import math

import jax
import jax.numpy as jnp
import numpy as np
from jax import lax
from jax.experimental import pallas as pl
from jax.experimental.pallas import tpu as pltpu
from jax.sharding import Mesh
from jax.sharding import PartitionSpec as P

ZL, Y, X, ZH, C = 8, 4, 4, 4, 2
AXES = ("zl", "y", "x", "zh", "c")
MERGE = 4
M = 32
PATCHES = M * MERGE
SOURCES = X * C
SLOTS = 2 * SOURCES
BASE = 10
REST = SLOTS - BASE
KB = MERGE * BASE
KR = MERGE * REST
HELD = MERGE * ZH * 2
ROWS = SOURCES * HELD
FULL = SOURCES * MERGE * 2
TAIL = 16
GROUPS, UNIT, UPAD = 3, 12, 16
BF = jnp.bfloat16
F32 = jnp.float32


def vmem():
    return pl.BlockSpec(memory_space=pltpu.VMEM)


def smem():
    return pl.BlockSpec(memory_space=pltpu.SMEM)


def nt(a, b):
    return lax.dot_general(a, b, (((1,), (1,)), ((), ())), preferred_element_type=F32)


def nn(a, b):
    return lax.dot_general(a, b, (((1,), (0,)), ((), ())), preferred_element_type=F32)


def iota(shape, dim):
    return lax.broadcasted_iota(jnp.int32, shape, dim)


def ones_where(mask):
    return jnp.where(mask, 1.0, 0.0).astype(BF)


def like(*shape, dtype=BF):
    return jax.ShapeDtypeStruct(shape, dtype)


def call(kernel, out, *args, scratch=()):
    several = isinstance(out, list)
    return pl.pallas_call(
        kernel,
        in_specs=[smem() if a.ndim == 1 else vmem() for a in args],
        out_specs=[vmem()] * len(out) if several else vmem(),
        out_shape=out,
        scratch_shapes=scratch,
        compiler_params=pltpu.CompilerParams(vmem_limit_bytes=32 << 20),
    )(*args)


def plane(o):
    return (o >> 1) & 3


def within(o):
    return ((o >> 3) << 1) + (o & 1)


def regroup_kernel(at, in_ref, *outs):
    width = outs[0].shape[-1]
    q, s = iota((ROWS, 64), 0), iota((ROWS, 64), 1)
    x, c = ((q >> 6) + at[0]) & 3, ((q >> 5) & 1) ^ at[1]
    source = (x << 4) + (((q >> 1) & 3) << 2) + (c << 1) + (q & 1)
    total = jnp.zeros((ROWS, width), F32)
    for k in range(MERGE):
        pick = ones_where((source == s) & (((q >> 3) & 3) == k))
        total += nn(pick, in_ref[0, :, k * width : (k + 1) * width])
    total = total.astype(BF)
    if len(outs) == 1:
        outs[0][...] = total.reshape(outs[0].shape)
    else:
        for i, out in enumerate(outs):
            out[...] = total[i * HELD : (i + 1) * HELD].reshape(out.shape)


def regroup(at, tap_slots, first, levels, width, apart):
    if apart:
        out = [like(levels, HELD, width)] * SOURCES
        specs = [pl.BlockSpec((1, HELD, width), lambda i: (i, 0, 0))] * SOURCES
    else:
        out = like(SOURCES, levels, HELD, width)
        specs = pl.BlockSpec((SOURCES, 1, HELD, width), lambda i: (0, i, 0, 0))
    return pl.pallas_call(
        regroup_kernel,
        grid=(levels,),
        in_specs=[smem(), pl.BlockSpec((1, 64, MERGE * width), lambda i: (first + i, 0, 0))],
        out_specs=specs,
        out_shape=out,
    )(at, tap_slots)


def deep_kernel(held, owners, out_ref):
    q, s = iota((ROWS, ROWS), 0), iota((ROWS, ROWS), 1)
    order = (((q >> 3) & 7) << 5) + (((q >> 1) & 3) << 3) + ((q >> 6) << 1) + (q & 1)
    rows = nn(ones_where(order == s), held[...].reshape(ROWS, held.shape[-1])).astype(BF)
    for zh in range(ZH):
        for j in range(rows.shape[1] // 128):
            out_ref[zh, j * FULL : (j + 1) * FULL, :] = rows[zh * FULL : (zh + 1) * FULL, j * 128 : (j + 1) * 128]
        last = rows.shape[1] // 128 * FULL
        out_ref[zh, last : last + TAIL, :] = jnp.broadcast_to(owners[...], (TAIL, 128)).astype(BF)


def own_kernel(owners, out_ref):
    patch, token = iota((PATCHES, 128), 0), iota((PATCHES, 128), 1)
    row = jnp.broadcast_to(owners[...].astype(jnp.int32), (PATCHES, 128))
    mine = token == (patch >> 2)
    o = jnp.sum(jnp.where(mine, row, 0), axis=1, keepdims=True)
    rank = jnp.sum(jnp.where((token < (patch >> 2)) & (row == o), 1, 0), axis=1, keepdims=True)
    at = (within(o) << 3) + ((iota((PATCHES, FULL), 0) & 3) << 1) + rank
    for zh in range(ZH):
        out_ref[zh] = ones_where((plane(o) == zh) & (at == iota((PATCHES, FULL), 1)))


def stream_kernel(at, take, got, upstream, out_ref, *turned):
    tap = []
    for j in range(upstream.shape[1] // 128):
        total = nn(take[0], got[0, j * FULL : (j + 1) * FULL, :])
        for zh in range(1, ZH):
            total += nn(take[zh], got[zh, j * FULL : (j + 1) * FULL, :])
        tap.append(total)
    scratch = turned[-1]
    for j, total in enumerate(tap):
        part = (upstream[:, j * 128 : (j + 1) * 128].astype(F32) + total).astype(BF)
        out_ref[:, j * 128 : (j + 1) * 128] = part
        scratch[j * 128 : (j + 1) * 128, :] = part.astype(F32).T.astype(BF)
    rows = scratch.shape[0] // X
    for d, out in enumerate(turned[:-1]):
        first = pl.multiple_of(((at[0] + d) & 3) * rows, 32)
        out[...] = scratch[pl.ds(first, rows), :]


def list_tables():
    table = np.zeros((8, ZH * (KB + KR)), np.int32)
    for first, count, start in ((0, BASE, 0), (BASE, REST, ZH * KB)):
        q = np.arange(ZH * MERGE * count)
        at = slice(start, start + q.size)
        table[0, at] = q // (MERGE * count)
        table[1, at] = q // count % MERGE
        table[2, at] = first + q % count
    return table


def route_kernel(at, got, table_ref, column_ref, pack_base, pack_rest, take_base, take_rest, over_ref):
    tokens = ZH * M
    here = at[2]
    last = got.shape[1] - TAIL
    lane = iota((TAIL, tokens), 1) >> 5
    owners = jnp.zeros((TAIL, tokens), F32)
    for zh in range(ZH):
        owners = jnp.where(lane == zh, got[zh, last : last + TAIL, :].astype(F32), owners)
    owners = owners[0:1].astype(jnp.int32)
    t_row, t_col = iota((tokens, tokens), 1), iota((tokens, tokens), 0)
    o_row = jnp.broadcast_to(owners, (tokens, tokens))
    o_col_1 = jnp.sum(jnp.where(t_row == t_col, o_row, 0), axis=1, keepdims=True)
    o_col = jnp.broadcast_to(o_col_1, (tokens, tokens))
    mates = (t_row >> 5) == (t_col >> 5)
    listed = mates & (plane(o_row) == plane(o_col))
    s_row, s_col = within(o_row), within(o_col)
    col_before = listed & ((s_row < s_col) | ((s_row == s_col) & (t_row < t_col)))
    row_before = listed & ((s_col < s_row) | ((s_col == s_row) & (t_col < t_row)))
    place_col = jnp.sum(jnp.where(col_before, 1, 0), axis=1, keepdims=True)
    place_row = jnp.sum(jnp.where(row_before, 1, 0), axis=0, keepdims=True)
    rank_col = jnp.sum(jnp.where(mates & (o_row == o_col) & (t_row < t_col), 1, 0), axis=1, keepdims=True)
    over_ref[...] = jnp.broadcast_to(jnp.max(place_row, axis=1, keepdims=True), over_ref.shape)

    n, nb = ZH * (KB + KR), ZH * KB
    entry = ones_where(
        (column_ref[:, 0:1] == (iota((n, tokens), 1) >> 5)) & (column_ref[:, 2:3] == place_row) & (plane(owners) == here)
    )
    row = iota((tokens, HELD), 1)
    held = (((row >> 1) & 3) == (iota((tokens, HELD), 0) >> 5)) & ((row & 1) == rank_col)
    same_k = column_ref[:, 1:2] == (iota((n, HELD), 1) >> 3)
    for source in range(SOURCES):
        pick = nn(entry, ones_where(held & (within(o_col_1) == source)))
        pick = jnp.where(same_k, pick, 0.0).astype(BF)
        pack_base[source] = pick[:nb]
        pack_rest[source] = pick[nb:]
    mine = ones_where(iota((PATCHES, tokens), 1) == here * M + (iota((PATCHES, tokens), 0) >> 2))

    def take(zh, first, count):
        q = table_ref[:, first : first + count]
        taken = nn(mine, ones_where((plane(o_col_1) == zh) & (q[2:3, :] == place_col)))
        return jnp.where(q[1:2, :] == (iota((PATCHES, count), 0) & 3), taken, 0.0).astype(BF)

    for zh in range(ZH):
        take_base[zh] = take(zh, zh * KB, KB)
        take_rest[zh] = take(zh, nb + zh * KR, KR)


def route(at, got):
    table = list_tables()
    out = [
        like(SOURCES, ZH * KB, HELD),
        like(SOURCES, ZH * KR, HELD),
        like(ZH, PATCHES, KB),
        like(ZH, PATCHES, KR),
        like(8, 128, dtype=jnp.int32),
    ]
    return call(route_kernel, out, at, got, jnp.asarray(table), jnp.asarray(table.T))


def pack_kernel(at, picks, *refs):
    held, out = refs[:-1], refs[-1]
    rows = out.shape[2]
    for level in range(out.shape[1]):
        total = None
        for i, ref in enumerate(held):
            source = (((at[0] - (i >> 1)) & 3) << 1) + ((i & 1) ^ at[1])
            part = nn(picks[source], ref[level])
            total = part if total is None else total + part
        for zh in range(ZH):
            out[zh, level] = total[zh * rows : (zh + 1) * rows].astype(BF)


def pack(at, picks, held):
    levels, _, width = held[0].shape
    return call(pack_kernel, like(ZH, levels, picks.shape[1] // ZH, width), at, picks, *held)


def shallow_kernel(take_base, take_rest, got, rest, out_ref):
    for level in range(out_ref.shape[0]):
        tap = nn(take_base[0], got[0, level]) + nn(take_rest[0], rest[0, level])
        for zh in range(1, ZH):
            tap += nn(take_base[zh], got[zh, level])
            tap += nn(take_rest[zh], rest[zh, level])
        out_ref[level] = tap.astype(BF)


def partial_kernel(at, a0, a1, a2, a3, s0, s1, s2, s3, place, mine, other, scratch):
    total = nt(a0[...], s0[...])
    for a, s in ((a1, s1), (a2, s2), (a3, s3)):
        total += nt(a[...], s[...])
    scratch[...] = total.astype(BF)
    rows = ZL * UPAD
    for d in range(Y):
        y = (at[3] + d) & 3
        block = None
        for g in range(GROUPS):
            first = pl.multiple_of((y * GROUPS + g) * rows, rows)
            part = nn(scratch[pl.ds(first, rows), :], place[g])
            block = part if block is None else block + part
        low, high = block[:, : ZH * 128], block[:, ZH * 128 :]
        first_core = at[1] == 0
        ours, theirs = jnp.where(first_core, low, high), jnp.where(first_core, high, low)
        for zh in range(ZH):
            mine[d, zh] = ours[:, zh * 128 : (zh + 1) * 128]
            other[d, zh] = theirs[:, zh * 128 : (zh + 1) * 128].astype(BF)


def sum_c_kernel(mine, got, own, *outs):
    own[...] = mine[0] + got[0].astype(F32)
    for d, out in enumerate(outs, 1):
        out[...] = (mine[d] + got[d].astype(F32)).astype(BF)


def sum_y_kernel(at, own, g1, g2, g3, *outs):
    scratch = outs[-1]
    total = own[...] + g1[...].astype(F32) + g2[...].astype(F32) + g3[...].astype(F32)
    for zl in range(ZL):
        scratch[zl] = total[:, zl * UPAD : (zl + 1) * UPAD, :]
    for d, out in enumerate(outs[:-1]):
        out[...] = scratch[(at[4] + d) & 7].astype(out.dtype)


def sum_zl_kernel(*refs):
    total = refs[0][...]
    for ref in refs[1:-1]:
        total += ref[...].astype(F32)
    refs[-1][...] = total.astype(BF)


def final_kernel(factor, got, out_ref):
    total = got[0].astype(F32)
    for i in range(1, ZH):
        total += got[i].astype(F32)
    total = total * factor
    for g in range(GROUPS):
        out_ref[g * UNIT : (g + 1) * UNIT, :] = total[:UNIT, g * 36 : (g + 1) * 36]


def fence(*arrays):
    return lax.optimization_barrier(arrays)


def exchange(x, axes):
    return lax.all_to_all(x, axes, 0, 0, tiled=True)


def shift(x, axis, by):
    n = lax.axis_size(axis)
    return lax.ppermute(x, axis, [(i, (i + by) % n) for i in range(n)])


def shift_xc(x, i):
    dx, dc = i >> 1, i & 1
    return lax.ppermute(x, ("x", "c"), [(a * C + b, (a + dx) % X * C + (b ^ dc)) for a in range(X) for b in range(C)])


def on_device(attention_out, upstream, tap_slots, owner_map, out_proj):
    width = attention_out.shape[1]
    factor = 1.0 / math.sqrt(PATCHES * ZL * Y * X * ZH * C)
    at = jnp.stack([lax.axis_index(a) for a in ("x", "c", "zh", "y", "zl")]).astype(jnp.int32)
    owners = jnp.tile(owner_map.reshape(1, M), (1, ZH)).astype(F32)

    q = np.arange(Y * GROUPS * ZL * UPAD)
    u, zl, g, y = q % UPAD, q // UPAD % ZL, q // (UPAD * ZL) % GROUPS, q // (UPAD * ZL * GROUPS)
    r_of = np.where(u < UNIT, zl * 144 + y * 36 + g * UNIT + u, -1)
    select = (jnp.asarray(r_of, jnp.int32)[:, None] == jnp.arange(width, dtype=jnp.int32)[None, :]).astype(BF)
    a_t = nt(select, attention_out).astype(BF)
    i, n = np.arange(288)[:, None], np.arange(C * ZH * 128)[None, :]
    j = [n % 128 - 36 * g for g in range(GROUPS)]
    place = np.stack([(i == (n // 128 % ZH) * 72 + (n // 512) * 36 + e) & (e >= 0) & (e < 36) for e in j])
    place = jnp.asarray(place.astype(np.float32), BF)

    held2 = exchange(regroup(jnp.zeros((4,), jnp.int32), tap_slots, 2, 1, width, False), ("x", "c"))
    take2 = call(own_kernel, like(ZH, PATCHES, FULL), owners)
    got2 = exchange(call(deep_kernel, like(ZH, width // 128 * FULL + TAIL, 128), held2, owners), "zh")
    held01 = regroup(at, tap_slots, 0, 2, width, True)
    held2, a_t, *held01 = fence(held2, a_t, *held01)
    held01 = [held01[0]] + [shift_xc(part, i) for i, part in enumerate(held01) if i]
    a_from = [a_t] + [shift(a_t, "x", d) for d in (1, 2, 3)]

    got2, take2, *a_from = fence(got2, take2, *a_from)
    pack_base, pack_rest, take_base, take_rest, over = route(at, got2)
    overflow = over[0, 0] >= BASE
    got01 = exchange(pack(at, pack_base, held01), "zh")

    turned = [like(width // X, PATCHES)] * X
    stream, *turned = call(
        stream_kernel, [like(PATCHES, width), *turned], at, take2, got2, upstream, scratch=[pltpu.VMEM((width, PATCHES), BF)]
    )
    s_from = [turned[0]] + [shift(turned[d], "x", d) for d in (1, 2, 3)]
    attention_grad = nt(stream, out_proj).astype(BF)
    block = (Y, ZH, ZL * UPAD, 128)
    mine, other = call(
        partial_kernel,
        [like(*block, dtype=F32), like(*block)],
        at,
        *a_from,
        *s_from,
        place,
        scratch=[pltpu.VMEM((a_t.shape[0], width // X), BF)],
    )
    own, *parts = call(sum_c_kernel, [like(*block[1:], dtype=F32)] + [like(*block[1:])] * 3, mine, shift(other, "c", 1))
    parts = [shift(part, "y", d) for d, part in enumerate(parts, 1)]
    block = (ZH, UPAD, 128)
    scratch = [pltpu.VMEM((ZL, *block), F32)]
    own, *parts = call(sum_y_kernel, [like(*block, dtype=F32)] + [like(*block)] * (ZL - 1), at, own, *parts, scratch=scratch)
    parts = [shift(part, "zl", d) for d, part in enumerate(parts, 1)]
    partial = call(sum_zl_kernel, like(*block), own, *parts)

    def second(picks, *held):
        return exchange(pack(at, picks, held), "zh")

    got01, pack_rest, partial = fence(got01, pack_rest, partial)
    rest = lax.cond(overflow, second, lambda picks, *held: jnp.zeros((ZH, 2, KR, width), BF), pack_rest, *held01)
    partial, rest = fence(partial, rest)
    proj_grad = call(functools.partial(final_kernel, factor), like(36, 36, dtype=F32), exchange(partial, "zh"))
    shallow = call(shallow_kernel, like(2, PATCHES, width), take_base, take_rest, got01, rest)
    return (stream, attention_grad, shallow, proj_grad)


def solution(mesh):
    fine = Mesh(mesh.devices.reshape(ZL, Y, X, ZH, C), AXES)
    dp, seq = ("zl", "y"), ("x", "zh", "c")
    in_specs = (P(AXES, None), P(AXES, None), P(None, AXES, None), P(AXES, None), P())
    out_specs = (P(AXES, None), P(AXES, None), P(None, AXES, None), P(dp, seq))
    return jax.shard_map(on_device, mesh=fine, in_specs=in_specs, out_specs=out_specs, check_vma=False)
```

```python
import functools
import math

import jax
import jax.numpy as jnp
import numpy as np
from jax import lax
from jax.experimental import pallas as pl
from jax.experimental.pallas import tpu as pltpu
from jax.sharding import Mesh
from jax.sharding import PartitionSpec as P

ZL, Y, X, ZH, C = 8, 4, 4, 4, 2
AXES = ("zl", "y", "x", "zh", "c")
MERGE = 4
M = 32
PATCHES = M * MERGE
SOURCES = X * C
SLOTS = 2 * SOURCES
BASE = 10
REST = SLOTS - BASE
KB = MERGE * BASE
KR = MERGE * REST
HELD = MERGE * ZH * 2
ROWS = SOURCES * HELD
FULL = SOURCES * MERGE * 2
TAIL = 16
GROUPS, UNIT, UPAD = 3, 12, 16
BF = jnp.bfloat16
F32 = jnp.float32


def vmem():
    return pl.BlockSpec(memory_space=pltpu.VMEM)


def smem():
    return pl.BlockSpec(memory_space=pltpu.SMEM)


def nt(a, b):
    return lax.dot_general(a, b, (((1,), (1,)), ((), ())), preferred_element_type=F32)


def nn(a, b):
    return lax.dot_general(a, b, (((1,), (0,)), ((), ())), preferred_element_type=F32)


def iota(shape, dim):
    return lax.broadcasted_iota(jnp.int32, shape, dim)


def ones_where(mask):
    return jnp.where(mask, 1.0, 0.0).astype(BF)


def like(*shape, dtype=BF):
    return jax.ShapeDtypeStruct(shape, dtype)


def call(kernel, out, *args, scratch=()):
    several = isinstance(out, list)
    return pl.pallas_call(
        kernel,
        in_specs=[smem() if a.ndim == 1 else vmem() for a in args],
        out_specs=[vmem()] * len(out) if several else vmem(),
        out_shape=out,
        scratch_shapes=scratch,
        compiler_params=pltpu.CompilerParams(vmem_limit_bytes=32 << 20),
    )(*args)


def plane(o):
    return (o >> 1) & 3


def within(o):
    return ((o >> 3) << 1) + (o & 1)


def regroup_kernel(at, in_ref, *outs):
    width = outs[0].shape[-1]
    q, s = iota((ROWS, 64), 0), iota((ROWS, 64), 1)
    x, c = ((q >> 6) + at[0]) & 3, ((q >> 5) & 1) ^ at[1]
    source = (x << 4) + (((q >> 1) & 3) << 2) + (c << 1) + (q & 1)
    total = jnp.zeros((ROWS, width), F32)
    for k in range(MERGE):
        pick = ones_where((source == s) & (((q >> 3) & 3) == k))
        total += nn(pick, in_ref[0, :, k * width : (k + 1) * width])
    total = total.astype(BF)
    if len(outs) == 1:
        outs[0][...] = total.reshape(outs[0].shape)
    else:
        for i, out in enumerate(outs):
            out[...] = total[i * HELD : (i + 1) * HELD].reshape(out.shape)


def regroup(at, tap_slots, first, levels, width, apart):
    if apart:
        out = [like(levels, HELD, width)] * SOURCES
        specs = [pl.BlockSpec((1, HELD, width), lambda i: (i, 0, 0))] * SOURCES
    else:
        out = like(SOURCES, levels, HELD, width)
        specs = pl.BlockSpec((SOURCES, 1, HELD, width), lambda i: (0, i, 0, 0))
    return pl.pallas_call(
        regroup_kernel,
        grid=(levels,),
        in_specs=[smem(), pl.BlockSpec((1, 64, MERGE * width), lambda i: (first + i, 0, 0))],
        out_specs=specs,
        out_shape=out,
    )(at, tap_slots)


def deep_kernel(held, owners, out_ref):
    q, s = iota((ROWS, ROWS), 0), iota((ROWS, ROWS), 1)
    order = (((q >> 3) & 7) << 5) + (((q >> 1) & 3) << 3) + ((q >> 6) << 1) + (q & 1)
    rows = nn(ones_where(order == s), held[...].reshape(ROWS, held.shape[-1])).astype(BF)
    for zh in range(ZH):
        for j in range(rows.shape[1] // 128):
            out_ref[zh, j * FULL : (j + 1) * FULL, :] = rows[zh * FULL : (zh + 1) * FULL, j * 128 : (j + 1) * 128]
        last = rows.shape[1] // 128 * FULL
        out_ref[zh, last : last + TAIL, :] = jnp.broadcast_to(owners[...], (TAIL, 128)).astype(BF)


def own_kernel(owners, out_ref):
    patch, token = iota((PATCHES, 128), 0), iota((PATCHES, 128), 1)
    row = jnp.broadcast_to(owners[...].astype(jnp.int32), (PATCHES, 128))
    mine = token == (patch >> 2)
    o = jnp.sum(jnp.where(mine, row, 0), axis=1, keepdims=True)
    rank = jnp.sum(jnp.where((token < (patch >> 2)) & (row == o), 1, 0), axis=1, keepdims=True)
    at = (within(o) << 3) + ((iota((PATCHES, FULL), 0) & 3) << 1) + rank
    for zh in range(ZH):
        out_ref[zh] = ones_where((plane(o) == zh) & (at == iota((PATCHES, FULL), 1)))


def stream_kernel(at, take, got, upstream, out_ref, *turned):
    tap = []
    for j in range(upstream.shape[1] // 128):
        total = nn(take[0], got[0, j * FULL : (j + 1) * FULL, :])
        for zh in range(1, ZH):
            total += nn(take[zh], got[zh, j * FULL : (j + 1) * FULL, :])
        tap.append(total)
    scratch = turned[-1]
    for j, total in enumerate(tap):
        part = (upstream[:, j * 128 : (j + 1) * 128].astype(F32) + total).astype(BF)
        out_ref[:, j * 128 : (j + 1) * 128] = part
        scratch[j * 128 : (j + 1) * 128, :] = part.astype(F32).T.astype(BF)
    rows = scratch.shape[0] // X
    for d, out in enumerate(turned[:-1]):
        first = pl.multiple_of(((at[0] + d) & 3) * rows, 32)
        out[...] = scratch[pl.ds(first, rows), :]


def list_tables():
    table = np.zeros((8, ZH * (KB + KR)), np.int32)
    for first, count, start in ((0, BASE, 0), (BASE, REST, ZH * KB)):
        q = np.arange(ZH * MERGE * count)
        at = slice(start, start + q.size)
        table[0, at] = q // (MERGE * count)
        table[1, at] = q // count % MERGE
        table[2, at] = first + q % count
    return table


def route_kernel(at, got, table_ref, column_ref, pack_base, pack_rest, take_base, take_rest, over_ref):
    tokens = ZH * M
    here = at[2]
    last = got.shape[1] - TAIL
    lane = iota((TAIL, tokens), 1) >> 5
    owners = jnp.zeros((TAIL, tokens), F32)
    for zh in range(ZH):
        owners = jnp.where(lane == zh, got[zh, last : last + TAIL, :].astype(F32), owners)
    owners = owners[0:1].astype(jnp.int32)
    t_row, t_col = iota((tokens, tokens), 1), iota((tokens, tokens), 0)
    o_row = jnp.broadcast_to(owners, (tokens, tokens))
    o_col_1 = jnp.sum(jnp.where(t_row == t_col, o_row, 0), axis=1, keepdims=True)
    o_col = jnp.broadcast_to(o_col_1, (tokens, tokens))
    mates = (t_row >> 5) == (t_col >> 5)
    listed = mates & (plane(o_row) == plane(o_col))
    s_row, s_col = within(o_row), within(o_col)
    col_before = listed & ((s_row < s_col) | ((s_row == s_col) & (t_row < t_col)))
    row_before = listed & ((s_col < s_row) | ((s_col == s_row) & (t_col < t_row)))
    place_col = jnp.sum(jnp.where(col_before, 1, 0), axis=1, keepdims=True)
    place_row = jnp.sum(jnp.where(row_before, 1, 0), axis=0, keepdims=True)
    rank_col = jnp.sum(jnp.where(mates & (o_row == o_col) & (t_row < t_col), 1, 0), axis=1, keepdims=True)
    over_ref[...] = jnp.broadcast_to(jnp.max(place_row, axis=1, keepdims=True), over_ref.shape)

    n, nb = ZH * (KB + KR), ZH * KB
    entry = ones_where(
        (column_ref[:, 0:1] == (iota((n, tokens), 1) >> 5)) & (column_ref[:, 2:3] == place_row) & (plane(owners) == here)
    )
    row = iota((tokens, HELD), 1)
    held = (((row >> 1) & 3) == (iota((tokens, HELD), 0) >> 5)) & ((row & 1) == rank_col)
    same_k = column_ref[:, 1:2] == (iota((n, HELD), 1) >> 3)
    for source in range(SOURCES):
        pick = nn(entry, ones_where(held & (within(o_col_1) == source)))
        pick = jnp.where(same_k, pick, 0.0).astype(BF)
        pack_base[source] = pick[:nb]
        pack_rest[source] = pick[nb:]
    mine = ones_where(iota((PATCHES, tokens), 1) == here * M + (iota((PATCHES, tokens), 0) >> 2))

    def take(zh, first, count):
        q = table_ref[:, first : first + count]
        taken = nn(mine, ones_where((plane(o_col_1) == zh) & (q[2:3, :] == place_col)))
        return jnp.where(q[1:2, :] == (iota((PATCHES, count), 0) & 3), taken, 0.0).astype(BF)

    for zh in range(ZH):
        take_base[zh] = take(zh, zh * KB, KB)
        take_rest[zh] = take(zh, nb + zh * KR, KR)


def route(at, got):
    table = list_tables()
    out = [
        like(SOURCES, ZH * KB, HELD),
        like(SOURCES, ZH * KR, HELD),
        like(ZH, PATCHES, KB),
        like(ZH, PATCHES, KR),
        like(8, 128, dtype=jnp.int32),
    ]
    return call(route_kernel, out, at, got, jnp.asarray(table), jnp.asarray(table.T))


def pack_kernel(at, picks, *refs):
    held, out = refs[:-1], refs[-1]
    rows = out.shape[2]
    for level in range(out.shape[1]):
        total = None
        for i, ref in enumerate(held):
            source = (((at[0] - (i >> 1)) & 3) << 1) + ((i & 1) ^ at[1])
            part = nn(picks[source], ref[level])
            total = part if total is None else total + part
        for zh in range(ZH):
            out[zh, level] = total[zh * rows : (zh + 1) * rows].astype(BF)


def pack(at, picks, held):
    levels, _, width = held[0].shape
    return call(pack_kernel, like(ZH, levels, picks.shape[1] // ZH, width), at, picks, *held)


def shallow_kernel(take_base, take_rest, got, rest, out_ref):
    for level in range(out_ref.shape[0]):
        tap = nn(take_base[0], got[0, level]) + nn(take_rest[0], rest[0, level])
        for zh in range(1, ZH):
            tap += nn(take_base[zh], got[zh, level])
            tap += nn(take_rest[zh], rest[zh, level])
        out_ref[level] = tap.astype(BF)


def partial_kernel(at, a0, a1, a2, a3, s0, s1, s2, s3, place, mine, other, scratch):
    total = nt(a0[...], s0[...])
    for a, s in ((a1, s1), (a2, s2), (a3, s3)):
        total += nt(a[...], s[...])
    scratch[...] = total.astype(BF)
    rows = ZL * UPAD
    for d in range(Y):
        y = (at[3] + d) & 3
        block = None
        for g in range(GROUPS):
            first = pl.multiple_of((y * GROUPS + g) * rows, rows)
            part = nn(scratch[pl.ds(first, rows), :], place[g])
            block = part if block is None else block + part
        low, high = block[:, : ZH * 128], block[:, ZH * 128 :]
        first_core = at[1] == 0
        ours, theirs = jnp.where(first_core, low, high), jnp.where(first_core, high, low)
        for zh in range(ZH):
            mine[d, zh] = ours[:, zh * 128 : (zh + 1) * 128]
            other[d, zh] = theirs[:, zh * 128 : (zh + 1) * 128].astype(BF)


def sum_c_kernel(mine, got, own, *outs):
    own[...] = mine[0] + got[0].astype(F32)
    for d, out in enumerate(outs, 1):
        out[...] = (mine[d] + got[d].astype(F32)).astype(BF)


def sum_y_kernel(at, own, g1, g2, g3, *outs):
    scratch = outs[-1]
    scratch[...] = own[...] + g1[...].astype(F32) + g2[...].astype(F32) + g3[...].astype(F32)
    for d, out in enumerate(outs[:-1]):
        out[...] = scratch[(at[2] + d) & 3].astype(out.dtype)


def sum_zh_kernel(own, g1, g2, g3, out_ref):
    total = own[...] + g1[...].astype(F32) + g2[...].astype(F32) + g3[...].astype(F32)
    out_ref[...] = total.astype(BF).reshape(out_ref.shape)


def final_kernel(factor, got, out_ref):
    total = got[0].astype(F32)
    for i in range(1, ZL):
        total += got[i].astype(F32)
    total = total * factor
    for g in range(GROUPS):
        out_ref[g * UNIT : (g + 1) * UNIT, :] = total[:UNIT, g * 36 : (g + 1) * 36]


def fence(*arrays):
    return lax.optimization_barrier(arrays)


def exchange(x, axes):
    return lax.all_to_all(x, axes, 0, 0, tiled=True)


def shift(x, axis, by):
    n = lax.axis_size(axis)
    return lax.ppermute(x, axis, [(i, (i + by) % n) for i in range(n)])


def shift_xc(x, i):
    dx, dc = i >> 1, i & 1
    return lax.ppermute(x, ("x", "c"), [(a * C + b, (a + dx) % X * C + (b ^ dc)) for a in range(X) for b in range(C)])


def on_device(attention_out, upstream, tap_slots, owner_map, out_proj):
    width = attention_out.shape[1]
    factor = 1.0 / math.sqrt(PATCHES * ZL * Y * X * ZH * C)
    at = jnp.stack([lax.axis_index(a) for a in ("x", "c", "zh", "y")]).astype(jnp.int32)
    owners = jnp.tile(owner_map.reshape(1, M), (1, ZH)).astype(F32)

    q = np.arange(Y * GROUPS * ZL * UPAD)
    u, zl, g, y = q % UPAD, q // UPAD % ZL, q // (UPAD * ZL) % GROUPS, q // (UPAD * ZL * GROUPS)
    r_of = np.where(u < UNIT, zl * 144 + y * 36 + g * UNIT + u, -1)
    select = (jnp.asarray(r_of, jnp.int32)[:, None] == jnp.arange(width, dtype=jnp.int32)[None, :]).astype(BF)
    a_t = nt(select, attention_out).astype(BF)
    i, n = np.arange(288)[:, None], np.arange(C * ZH * 128)[None, :]
    j = [n % 128 - 36 * g for g in range(GROUPS)]
    place = np.stack([(i == (n // 128 % ZH) * 72 + (n // 512) * 36 + e) & (e >= 0) & (e < 36) for e in j])
    place = jnp.asarray(place.astype(np.float32), BF)

    held2 = exchange(regroup(jnp.zeros((4,), jnp.int32), tap_slots, 2, 1, width, False), ("x", "c"))
    take2 = call(own_kernel, like(ZH, PATCHES, FULL), owners)
    got2 = exchange(call(deep_kernel, like(ZH, width // 128 * FULL + TAIL, 128), held2, owners), "zh")
    held01 = regroup(at, tap_slots, 0, 2, width, True)
    held2, a_t, *held01 = fence(held2, a_t, *held01)
    held01 = [held01[0]] + [shift_xc(part, i) for i, part in enumerate(held01) if i]
    a_from = [a_t] + [shift(a_t, "x", d) for d in (1, 2, 3)]

    got2, take2, *a_from = fence(got2, take2, *a_from)
    pack_base, pack_rest, take_base, take_rest, over = route(at, got2)
    overflow = over[0, 0] >= BASE
    got01 = exchange(pack(at, pack_base, held01), "zh")

    turned = [like(width // X, PATCHES)] * X
    stream, *turned = call(
        stream_kernel, [like(PATCHES, width), *turned], at, take2, got2, upstream, scratch=[pltpu.VMEM((width, PATCHES), BF)]
    )
    s_from = [turned[0]] + [shift(turned[d], "x", d) for d in (1, 2, 3)]
    attention_grad = nt(stream, out_proj).astype(BF)
    block = (Y, ZH, ZL * UPAD, 128)
    mine, other = call(
        partial_kernel,
        [like(*block, dtype=F32), like(*block)],
        at,
        *a_from,
        *s_from,
        place,
        scratch=[pltpu.VMEM((a_t.shape[0], width // X), BF)],
    )
    own, *parts = call(sum_c_kernel, [like(*block[1:], dtype=F32)] + [like(*block[1:])] * 3, mine, shift(other, "c", 1))
    parts = [shift(part, "y", d) for d, part in enumerate(parts, 1)]
    block = (ZL * UPAD, 128)
    scratch = [pltpu.VMEM((ZH, *block), F32)]
    own, *parts = call(sum_y_kernel, [like(*block, dtype=F32)] + [like(*block)] * 3, at, own, *parts, scratch=scratch)
    parts = [shift(part, "zh", d) for d, part in enumerate(parts, 1)]
    partial = call(sum_zh_kernel, like(ZL, UPAD, 128), own, *parts)

    def second(picks, *held):
        return exchange(pack(at, picks, held), "zh")

    got01, pack_rest, partial = fence(got01, pack_rest, partial)
    rest = lax.cond(overflow, second, lambda picks, *held: jnp.zeros((ZH, 2, KR, width), BF), pack_rest, *held01)
    partial, rest = fence(partial, rest)
    proj_grad = call(functools.partial(final_kernel, factor), like(36, 36, dtype=F32), exchange(partial, "zl"))
    shallow = call(shallow_kernel, like(2, PATCHES, width), take_base, take_rest, got01, rest)
    return (stream, attention_grad, shallow, proj_grad)


def solution(mesh):
    fine = Mesh(mesh.devices.reshape(ZL, Y, X, ZH, C), AXES)
    dp, seq = ("zl", "y"), ("x", "zh", "c")
    in_specs = (P(AXES, None), P(AXES, None), P(None, AXES, None), P(AXES, None), P())
    out_specs = (P(AXES, None), P(AXES, None), P(None, AXES, None), P(dp, seq))
    return jax.shard_map(on_device, mesh=fine, in_specs=in_specs, out_specs=out_specs, check_vma=False)
```

```python
import functools
import math

import jax
import jax.numpy as jnp
import numpy as np
from jax import lax
from jax.experimental import pallas as pl
from jax.experimental.pallas import tpu as pltpu
from jax.sharding import Mesh
from jax.sharding import PartitionSpec as P

ZL, Y, X, ZH, C = 8, 4, 4, 4, 2
AXES = ("zl", "y", "x", "zh", "c")
MERGE = 4
M = 32
PATCHES = M * MERGE
SOURCES = X * C
SLOTS = 2 * SOURCES
BASE = 10
REST = SLOTS - BASE
KB = MERGE * BASE
KR = MERGE * REST
HELD = MERGE * ZH * 2
ROWS = SOURCES * HELD
FULL = SOURCES * MERGE * 2
TAIL = 16
GROUPS, UNIT, UPAD = 3, 12, 16
BF = jnp.bfloat16
F32 = jnp.float32


def vmem():
    return pl.BlockSpec(memory_space=pltpu.VMEM)


def smem():
    return pl.BlockSpec(memory_space=pltpu.SMEM)


def nt(a, b):
    return lax.dot_general(a, b, (((1,), (1,)), ((), ())), preferred_element_type=F32)


def nn(a, b):
    return lax.dot_general(a, b, (((1,), (0,)), ((), ())), preferred_element_type=F32)


def iota(shape, dim):
    return lax.broadcasted_iota(jnp.int32, shape, dim)


def ones_where(mask):
    return jnp.where(mask, 1.0, 0.0).astype(BF)


def like(*shape, dtype=BF):
    return jax.ShapeDtypeStruct(shape, dtype)


def call(kernel, out, *args, scratch=()):
    several = isinstance(out, list)
    return pl.pallas_call(
        kernel,
        in_specs=[smem() if a.ndim == 1 else vmem() for a in args],
        out_specs=[vmem()] * len(out) if several else vmem(),
        out_shape=out,
        scratch_shapes=scratch,
        compiler_params=pltpu.CompilerParams(vmem_limit_bytes=32 << 20),
    )(*args)


def plane(o):
    return (o >> 1) & 3


def within(o):
    return ((o >> 3) << 1) + (o & 1)


def regroup_kernel(at, in_ref, *outs):
    width = outs[0].shape[-1]
    q, s = iota((ROWS, 64), 0), iota((ROWS, 64), 1)
    x, c = ((q >> 6) + at[0]) & 3, ((q >> 5) & 1) ^ at[1]
    source = (x << 4) + (((q >> 1) & 3) << 2) + (c << 1) + (q & 1)
    total = jnp.zeros((ROWS, width), F32)
    for k in range(MERGE):
        pick = ones_where((source == s) & (((q >> 3) & 3) == k))
        total += nn(pick, in_ref[0, :, k * width : (k + 1) * width])
    total = total.astype(BF)
    if len(outs) == 1:
        outs[0][...] = total.reshape(outs[0].shape)
    else:
        for i, out in enumerate(outs):
            out[...] = total[i * HELD : (i + 1) * HELD].reshape(out.shape)


def regroup(at, tap_slots, first, levels, width, apart):
    if apart:
        out = [like(levels, HELD, width)] * SOURCES
        specs = [pl.BlockSpec((1, HELD, width), lambda i: (i, 0, 0))] * SOURCES
    else:
        out = like(SOURCES, levels, HELD, width)
        specs = pl.BlockSpec((SOURCES, 1, HELD, width), lambda i: (0, i, 0, 0))
    return pl.pallas_call(
        regroup_kernel,
        grid=(levels,),
        in_specs=[smem(), pl.BlockSpec((1, 64, MERGE * width), lambda i: (first + i, 0, 0))],
        out_specs=specs,
        out_shape=out,
    )(at, tap_slots)


def deep_kernel(held, owners, out_ref):
    q, s = iota((ROWS, ROWS), 0), iota((ROWS, ROWS), 1)
    order = (((q >> 3) & 7) << 5) + (((q >> 1) & 3) << 3) + ((q >> 6) << 1) + (q & 1)
    rows = nn(ones_where(order == s), held[...].reshape(ROWS, held.shape[-1])).astype(BF)
    for zh in range(ZH):
        for j in range(rows.shape[1] // 128):
            out_ref[zh, j * FULL : (j + 1) * FULL, :] = rows[zh * FULL : (zh + 1) * FULL, j * 128 : (j + 1) * 128]
        last = rows.shape[1] // 128 * FULL
        out_ref[zh, last : last + TAIL, :] = jnp.broadcast_to(owners[...], (TAIL, 128)).astype(BF)


def own_kernel(owners, out_ref):
    patch, token = iota((PATCHES, 128), 0), iota((PATCHES, 128), 1)
    row = jnp.broadcast_to(owners[...].astype(jnp.int32), (PATCHES, 128))
    mine = token == (patch >> 2)
    o = jnp.sum(jnp.where(mine, row, 0), axis=1, keepdims=True)
    rank = jnp.sum(jnp.where((token < (patch >> 2)) & (row == o), 1, 0), axis=1, keepdims=True)
    at = (within(o) << 3) + ((iota((PATCHES, FULL), 0) & 3) << 1) + rank
    for zh in range(ZH):
        out_ref[zh] = ones_where((plane(o) == zh) & (at == iota((PATCHES, FULL), 1)))


def stream_kernel(at, take, got, upstream, out_ref, *turned):
    tap = []
    for j in range(upstream.shape[1] // 128):
        total = nn(take[0], got[0, j * FULL : (j + 1) * FULL, :])
        for zh in range(1, ZH):
            total += nn(take[zh], got[zh, j * FULL : (j + 1) * FULL, :])
        tap.append(total)
    scratch = turned[-1]
    for j, total in enumerate(tap):
        part = (upstream[:, j * 128 : (j + 1) * 128].astype(F32) + total).astype(BF)
        out_ref[:, j * 128 : (j + 1) * 128] = part
        scratch[j * 128 : (j + 1) * 128, :] = part.astype(F32).T.astype(BF)
    rows = scratch.shape[0] // X
    for d, out in enumerate(turned[:-1]):
        first = pl.multiple_of(((at[0] + d) & 3) * rows, 32)
        out[...] = scratch[pl.ds(first, rows), :]


def list_tables():
    table = np.zeros((8, ZH * (KB + KR)), np.int32)
    for first, count, start in ((0, BASE, 0), (BASE, REST, ZH * KB)):
        q = np.arange(ZH * MERGE * count)
        at = slice(start, start + q.size)
        table[0, at] = q // (MERGE * count)
        table[1, at] = q // count % MERGE
        table[2, at] = first + q % count
    return table


def route_kernel(at, got, table_ref, column_ref, pack_base, pack_rest, take_base, take_rest, over_ref):
    tokens = ZH * M
    here = at[2]
    last = got.shape[1] - TAIL
    lane = iota((TAIL, tokens), 1) >> 5
    owners = jnp.zeros((TAIL, tokens), F32)
    for zh in range(ZH):
        owners = jnp.where(lane == zh, got[zh, last : last + TAIL, :].astype(F32), owners)
    owners = owners[0:1].astype(jnp.int32)
    t_row, t_col = iota((tokens, tokens), 1), iota((tokens, tokens), 0)
    o_row = jnp.broadcast_to(owners, (tokens, tokens))
    o_col_1 = jnp.sum(jnp.where(t_row == t_col, o_row, 0), axis=1, keepdims=True)
    o_col = jnp.broadcast_to(o_col_1, (tokens, tokens))
    mates = (t_row >> 5) == (t_col >> 5)
    listed = mates & (plane(o_row) == plane(o_col))
    s_row, s_col = within(o_row), within(o_col)
    col_before = listed & ((s_row < s_col) | ((s_row == s_col) & (t_row < t_col)))
    row_before = listed & ((s_col < s_row) | ((s_col == s_row) & (t_col < t_row)))
    place_col = jnp.sum(jnp.where(col_before, 1, 0), axis=1, keepdims=True)
    place_row = jnp.sum(jnp.where(row_before, 1, 0), axis=0, keepdims=True)
    rank_col = jnp.sum(jnp.where(mates & (o_row == o_col) & (t_row < t_col), 1, 0), axis=1, keepdims=True)
    over_ref[...] = jnp.broadcast_to(jnp.max(place_row, axis=1, keepdims=True), over_ref.shape)

    n, nb = ZH * (KB + KR), ZH * KB
    entry = ones_where(
        (column_ref[:, 0:1] == (iota((n, tokens), 1) >> 5)) & (column_ref[:, 2:3] == place_row) & (plane(owners) == here)
    )
    row = iota((tokens, HELD), 1)
    held = (((row >> 1) & 3) == (iota((tokens, HELD), 0) >> 5)) & ((row & 1) == rank_col)
    same_k = column_ref[:, 1:2] == (iota((n, HELD), 1) >> 3)
    for source in range(SOURCES):
        pick = nn(entry, ones_where(held & (within(o_col_1) == source)))
        pick = jnp.where(same_k, pick, 0.0).astype(BF)
        pack_base[source] = pick[:nb]
        pack_rest[source] = pick[nb:]
    mine = ones_where(iota((PATCHES, tokens), 1) == here * M + (iota((PATCHES, tokens), 0) >> 2))

    def take(zh, first, count):
        q = table_ref[:, first : first + count]
        taken = nn(mine, ones_where((plane(o_col_1) == zh) & (q[2:3, :] == place_col)))
        return jnp.where(q[1:2, :] == (iota((PATCHES, count), 0) & 3), taken, 0.0).astype(BF)

    for zh in range(ZH):
        take_base[zh] = take(zh, zh * KB, KB)
        take_rest[zh] = take(zh, nb + zh * KR, KR)


def route(at, got):
    table = list_tables()
    out = [
        like(SOURCES, ZH * KB, HELD),
        like(SOURCES, ZH * KR, HELD),
        like(ZH, PATCHES, KB),
        like(ZH, PATCHES, KR),
        like(8, 128, dtype=jnp.int32),
    ]
    return call(route_kernel, out, at, got, jnp.asarray(table), jnp.asarray(table.T))


def pack_kernel(at, picks, *refs):
    held, out = refs[:-1], refs[-1]
    rows = out.shape[2]
    for level in range(out.shape[1]):
        total = None
        for i, ref in enumerate(held):
            source = (((at[0] - (i >> 1)) & 3) << 1) + ((i & 1) ^ at[1])
            part = nn(picks[source], ref[level])
            total = part if total is None else total + part
        for zh in range(ZH):
            out[zh, level] = total[zh * rows : (zh + 1) * rows].astype(BF)


def pack(at, picks, held):
    levels, _, width = held[0].shape
    return call(pack_kernel, like(ZH, levels, picks.shape[1] // ZH, width), at, picks, *held)


def shallow_kernel(take_base, take_rest, got, rest, out_ref):
    for level in range(out_ref.shape[0]):
        tap = nn(take_base[0], got[0, level]) + nn(take_rest[0], rest[0, level])
        for zh in range(1, ZH):
            tap += nn(take_base[zh], got[zh, level])
            tap += nn(take_rest[zh], rest[zh, level])
        out_ref[level] = tap.astype(BF)


def partial_kernel(at, a0, a1, a2, a3, s0, s1, s2, s3, place, mine, other, scratch):
    total = nt(a0[...], s0[...])
    for a, s in ((a1, s1), (a2, s2), (a3, s3)):
        total += nt(a[...], s[...])
    scratch[...] = total.astype(BF)
    rows = ZL * UPAD
    for d in range(Y):
        y = (at[3] + d) & 3
        block = None
        for g in range(GROUPS):
            first = pl.multiple_of((y * GROUPS + g) * rows, rows)
            part = nn(scratch[pl.ds(first, rows), :], place[g])
            block = part if block is None else block + part
        low, high = block[:, : ZH * 128], block[:, ZH * 128 :]
        first_core = at[1] == 0
        ours, theirs = jnp.where(first_core, low, high), jnp.where(first_core, high, low)
        for zh in range(ZH):
            mine[d, zh] = ours[:, zh * 128 : (zh + 1) * 128]
            other[d, zh] = theirs[:, zh * 128 : (zh + 1) * 128].astype(BF)


def sum_c_kernel(mine, got, own, *outs):
    own[...] = mine[0] + got[0].astype(F32)
    for d, out in enumerate(outs, 1):
        out[...] = (mine[d] + got[d].astype(F32)).astype(BF)


def sum_y_kernel(at, own, g1, g2, g3, keep, send, scratch):
    scratch[...] = own[...] + g1[...].astype(F32) + g2[...].astype(F32) + g3[...].astype(F32)
    for d in range(2):
        keep[d] = scratch[at[2] ^ d]
        send[d] = scratch[at[2] ^ 2 ^ d].astype(BF)


def sum_far_kernel(keep, got, mine, send):
    mine[...] = keep[0] + got[0].astype(F32)
    send[...] = keep[1] + got[1].astype(F32)


def sum_near_kernel(mine, got, out_ref):
    out_ref[...] = (mine[...] + got[...]).astype(BF).reshape(out_ref.shape)


def final_kernel(factor, got, out_ref):
    total = got[0].astype(F32)
    for i in range(1, ZL):
        total += got[i].astype(F32)
    total = total * factor
    for g in range(GROUPS):
        out_ref[g * UNIT : (g + 1) * UNIT, :] = total[:UNIT, g * 36 : (g + 1) * 36]


def fence(*arrays):
    return lax.optimization_barrier(arrays)


def exchange(x, axes):
    return lax.all_to_all(x, axes, 0, 0, tiled=True)


def shift(x, axis, by):
    n = lax.axis_size(axis)
    return lax.ppermute(x, axis, [(i, (i + by) % n) for i in range(n)])


def swap(x, bit):
    return lax.ppermute(x, "zh", [(i, i ^ bit) for i in range(ZH)])


def shift_xc(x, i):
    dx, dc = i >> 1, i & 1
    return lax.ppermute(x, ("x", "c"), [(a * C + b, (a + dx) % X * C + (b ^ dc)) for a in range(X) for b in range(C)])


def on_device(attention_out, upstream, tap_slots, owner_map, out_proj):
    width = attention_out.shape[1]
    factor = 1.0 / math.sqrt(PATCHES * ZL * Y * X * ZH * C)
    at = jnp.stack([lax.axis_index(a) for a in ("x", "c", "zh", "y")]).astype(jnp.int32)
    owners = jnp.tile(owner_map.reshape(1, M), (1, ZH)).astype(F32)

    q = np.arange(Y * GROUPS * ZL * UPAD)
    u, zl, g, y = q % UPAD, q // UPAD % ZL, q // (UPAD * ZL) % GROUPS, q // (UPAD * ZL * GROUPS)
    r_of = np.where(u < UNIT, zl * 144 + y * 36 + g * UNIT + u, -1)
    select = (jnp.asarray(r_of, jnp.int32)[:, None] == jnp.arange(width, dtype=jnp.int32)[None, :]).astype(BF)
    a_t = nt(select, attention_out).astype(BF)
    i, n = np.arange(288)[:, None], np.arange(C * ZH * 128)[None, :]
    j = [n % 128 - 36 * g for g in range(GROUPS)]
    place = np.stack([(i == (n // 128 % ZH) * 72 + (n // 512) * 36 + e) & (e >= 0) & (e < 36) for e in j])
    place = jnp.asarray(place.astype(np.float32), BF)

    held2 = exchange(regroup(jnp.zeros((4,), jnp.int32), tap_slots, 2, 1, width, False), ("x", "c"))
    take2 = call(own_kernel, like(ZH, PATCHES, FULL), owners)
    got2 = exchange(call(deep_kernel, like(ZH, width // 128 * FULL + TAIL, 128), held2, owners), "zh")
    held01 = regroup(at, tap_slots, 0, 2, width, True)
    held2, a_t, *held01 = fence(held2, a_t, *held01)
    held01 = [held01[0]] + [shift_xc(part, i) for i, part in enumerate(held01) if i]
    a_from = [a_t] + [shift(a_t, "x", d) for d in (1, 2, 3)]

    got2, take2, *a_from = fence(got2, take2, *a_from)
    pack_base, pack_rest, take_base, take_rest, over = route(at, got2)
    overflow = over[0, 0] >= BASE
    got01 = exchange(pack(at, pack_base, held01), "zh")

    turned = [like(width // X, PATCHES)] * X
    stream, *turned = call(
        stream_kernel, [like(PATCHES, width), *turned], at, take2, got2, upstream, scratch=[pltpu.VMEM((width, PATCHES), BF)]
    )
    s_from = [turned[0]] + [shift(turned[d], "x", d) for d in (1, 2, 3)]
    attention_grad = nt(stream, out_proj).astype(BF)
    block = (Y, ZH, ZL * UPAD, 128)
    mine, other = call(
        partial_kernel,
        [like(*block, dtype=F32), like(*block)],
        at,
        *a_from,
        *s_from,
        place,
        scratch=[pltpu.VMEM((a_t.shape[0], width // X), BF)],
    )
    own, *parts = call(sum_c_kernel, [like(*block[1:], dtype=F32)] + [like(*block[1:])] * 3, mine, shift(other, "c", 1))
    parts = [shift(part, "y", d) for d, part in enumerate(parts, 1)]
    block = (ZL * UPAD, 128)
    scratch = [pltpu.VMEM((ZH, *block), F32)]
    out = [like(2, *block, dtype=F32), like(2, *block)]
    keep, send = call(sum_y_kernel, out, at, own, *parts, scratch=scratch)
    own, send = call(sum_far_kernel, [like(*block, dtype=F32)] * 2, keep, swap(send, 2))
    partial = call(sum_near_kernel, like(ZL, UPAD, 128), own, swap(send, 1))

    def second(picks, *held):
        return exchange(pack(at, picks, held), "zh")

    got01, pack_rest, partial = fence(got01, pack_rest, partial)
    rest = lax.cond(overflow, second, lambda picks, *held: jnp.zeros((ZH, 2, KR, width), BF), pack_rest, *held01)
    partial, rest = fence(partial, rest)
    proj_grad = call(functools.partial(final_kernel, factor), like(36, 36, dtype=F32), exchange(partial, "zl"))
    shallow = call(shallow_kernel, like(2, PATCHES, width), take_base, take_rest, got01, rest)
    return (stream, attention_grad, shallow, proj_grad)


def solution(mesh):
    fine = Mesh(mesh.devices.reshape(ZL, Y, X, ZH, C), AXES)
    dp, seq = ("zl", "y"), ("x", "zh", "c")
    in_specs = (P(AXES, None), P(AXES, None), P(None, AXES, None), P(AXES, None), P())
    out_specs = (P(AXES, None), P(AXES, None), P(None, AXES, None), P(dp, seq))
    return jax.shard_map(on_device, mesh=fine, in_specs=in_specs, out_specs=out_specs, check_vma=False)
```
